256 devices in a mesh: replica: 16 (over z_hi, y, core), tp: 16 (over z_lo, x).
Axes of the slice: x: 4, y: 4, z: 8 (z_hi: 2, z_lo: 4; z = z_hi * 4 + z_lo), core: 2. Of those that a mesh axis runs over, the one named last changes fastest.
Arguments:
- weight_delta: bfloat16 [2048, 5120], P('tp', 'replica'), may hold values from -4 to 4
- rollout_copy: bfloat16 [16, 2048, 5120], P('replica', 'tp'), may hold values from -1.5 to 1.5
- cached_inputs: bfloat16 [32768, 5120], P('replica'), may hold values from -0.078125 to 0.078125
Outputs:
- renewed_weights: bfloat16 [16, 2048, 5120], P('replica', 'tp')
- keys_values: bfloat16 [32768, 2048], P('replica', 'tp')
The draws below stay inside these ranges and needn't reach their ends.
All inputs are finite; a program needn't handle non-finite values.
Results may differ from the reference program's by a relative error of at most 0.0056.
Values may be sent and summed in bfloat16 or wider, within the bound.
No kernel may reach another device: no remote copies, remote signals or barrier semaphores. Data moves between devices by JAX's collectives and lax.ppermute only.
A program may use at most 64 MiB of HBM per device.

```python
import math
import jax
import jax.numpy as jnp
from jax import lax

D = 5120
TILE = 128
TOK_REP = 2048
KV_OUT = 2048
TOKENS = 32768
N_REPLICA = 16


def draw_weight_delta(key, part):
    key = jax.random.fold_in(key, 7)
    first_key, second_key = jax.random.split(key, 2)
    grid_shape = (KV_OUT // TILE, D // TILE)
    tile_level = jnp.exp(jax.random.uniform(second_key, grid_shape, jnp.float32, math.log(0.25), 0.0))
    values = jnp.clip(jax.random.normal(first_key, (KV_OUT, D), jnp.float32), -4.0, 4.0)
    spread = jnp.repeat(jnp.repeat(tile_level, TILE, axis=0), TILE, axis=1)
    return (values * spread).astype(jnp.bfloat16)


def levels(own_key, dims, cuts, low, high):
    gain, own = 1.0, jax.random.fold_in(own_key, 6)
    for dim, shards_of in cuts:
        steps = jnp.exp(jax.random.uniform(jax.random.fold_in(own, dim), (shards_of,), jnp.float32, low / len(cuts), high / len(cuts)))
        gain = gain * jnp.repeat(steps, dims[dim] // shards_of).reshape([-1 if axis == dim else 1 for axis in range(len(dims))])
    return gain


def normal_values(rng, dims, scale, bound, cuts=(), kind=jnp.bfloat16):
    drawn = scale * jax.random.normal(rng, dims, jnp.float32)
    if cuts:
        drawn = drawn * levels(rng, dims, cuts, -0.22, 0.18)
    return jnp.clip(drawn, -bound, bound).astype(kind)


def setup_inputs(seed: int = 0) -> dict:
    arg_keys = jax.random.split(jax.random.key(seed), 4)
    weight_delta = draw_weight_delta(jax.random.fold_in(arg_keys[3], 71), 0)
    rollout_copy = normal_values(arg_keys[1], (N_REPLICA, KV_OUT, D), 0.25, 1.5, ((0, 16), (1, 16)))
    cached_inputs = normal_values(arg_keys[2], (TOKENS, D), 0.014, 0.078125, ((0, 16),))
    return dict(weight_delta=weight_delta, rollout_copy=rollout_copy, cached_inputs=cached_inputs)


EPSILON = 1e-6


def tile_scale_full(values):
    magnitude = jnp.abs(values.astype(jnp.float32))
    row_count, col_count = magnitude.shape
    blocks = magnitude.reshape(row_count // TILE, TILE, col_count // TILE, TILE)
    peak = jnp.max(blocks, axis=(1, 3)) + EPSILON
    return jnp.repeat(jnp.repeat(peak, TILE, axis=0), TILE, axis=1)


def reference(weight_delta, rollout_copy, cached_inputs):
    scale_grid = tile_scale_full(weight_delta)
    quantized = (weight_delta.astype(jnp.float32) / scale_grid).astype(jnp.bfloat16)
    quantized = lax.optimization_barrier(quantized)
    restored = quantized.astype(jnp.float32) * scale_grid

    def per_replica(pair_items):
        copy_block, token_block = pair_items
        renewed = (copy_block.astype(jnp.float32) + restored).astype(jnp.bfloat16)
        projected = lax.dot_general(token_block, renewed, (((1,), (1,)), ((), ())), preferred_element_type=jnp.float32)
        return renewed, projected.astype(jnp.bfloat16)

    token_groups = cached_inputs.reshape(N_REPLICA, TOK_REP, D)
    renewed_all, projected_all = lax.map(per_replica, (rollout_copy, token_groups))
    return renewed_all, projected_all.reshape(TOKENS, KV_OUT)
```

```python
import functools

import jax
import jax.numpy as jnp
from jax import lax
from jax.experimental import pallas as pl
from jax.experimental.pallas import tpu as pltpu
from jax.sharding import PartitionSpec as P

TILE = 128
EPSILON = 1e-06
STEPS = (2, 1, 3)
TOKEN_BLOCK = 512

NT = (((1,), (1,)), ((), ()))


def moved(dz=0, dy=0, dc=0):
    pairs = []
    for source in range(16):
        z, y, core = source >> 3, (source >> 1) & 3, source & 1
        pairs.append((source, ((z + dz) % 2) * 8 + ((y + dy) % 4) * 2 + (core + dc) % 2))
    return pairs


def send(value, **offset):
    return lax.ppermute(value, "replica", moved(**offset))


def whereabouts():
    replica = lax.axis_index("replica")
    return replica >> 3, (replica >> 1) & 3, replica & 1


def renew_half(place, pieces, swapped, held, delta, weights, half):
    piece_rows = pieces[0].shape[0]
    half_width = delta.shape[0]
    _, y, core = place
    for index, step in enumerate((0,) + STEPS):
        chip = lax.rem(y + 4 - step, 4)
        base = chip * (2 * piece_rows)
        mine = pl.multiple_of(base + core * piece_rows, 64)
        other = pl.multiple_of(base + (1 - core) * piece_rows, 64)
        delta[pl.ds(mine, piece_rows), :] = pieces[index][...]
        delta[pl.ds(other, piece_rows), :] = swapped[index * piece_rows : (index + 1) * piece_rows, :]
    row = lax.broadcasted_iota(jnp.int32, (TILE, TILE), 0)
    col = lax.broadcasted_iota(jnp.int32, (TILE, TILE), 1)
    identity = (row == col).astype(jnp.bfloat16)
    start = half * half_width
    for t in range(half_width // TILE):
        tile = delta[t * TILE : (t + 1) * TILE, :].astype(jnp.float32)
        scale = jnp.max(jnp.abs(tile), axis=(0, 1), keepdims=True) + EPSILON
        normalized = (tile / scale).astype(jnp.bfloat16)
        turned = lax.dot_general(identity, normalized, NT, preferred_element_type=jnp.float32)
        columns = pl.ds(pl.multiple_of(start + t * TILE, TILE), TILE)
        fresh = held[:, columns].astype(jnp.float32) + turned * scale
        weights[:, t * TILE : (t + 1) * TILE] = fresh.astype(jnp.bfloat16)


def first_kernel(p0, p1, p2, p3, swapped, held, tokens, weights, partial, delta):
    place = whereabouts()
    half = place[0]
    renew_half(place, (p0, p1, p2, p3), swapped, held, delta, weights, half)
    width = weights.shape[1]
    columns = pl.ds(pl.multiple_of(half * width, TILE), width)

    @pl.loop(0, tokens.shape[0] // TOKEN_BLOCK)
    def _(block):
        rows = pl.ds(pl.multiple_of(block * TOKEN_BLOCK, TOKEN_BLOCK), TOKEN_BLOCK)
        partial[rows, :] = lax.dot_general(
            tokens[rows, columns], weights[...], NT, preferred_element_type=jnp.float32
        )


def second_kernel(
    p0, p1, p2, p3, swapped, held, tokens, near_weights, partial,
    renewed, result, delta, far_weights, near_sem, far_sem,
):
    place = whereabouts()
    near, far = place[0], 1 - place[0]
    width = far_weights.shape[1]
    near_columns = pl.ds(pl.multiple_of(near * width, TILE), width)
    far_columns = pl.ds(pl.multiple_of(far * width, TILE), width)
    near_copy = pltpu.make_async_copy(near_weights, renewed.at[:, near_columns], near_sem)
    near_copy.start()
    renew_half(place, (p0, p1, p2, p3), swapped, held, delta, far_weights, far)
    far_copy = pltpu.make_async_copy(far_weights, renewed.at[:, far_columns], far_sem)
    far_copy.start()

    @pl.loop(0, tokens.shape[0] // TOKEN_BLOCK)
    def _(block):
        rows = pl.ds(pl.multiple_of(block * TOKEN_BLOCK, TOKEN_BLOCK), TOKEN_BLOCK)
        result[rows, :] = (
            partial[rows, :]
            + lax.dot_general(
                tokens[rows, far_columns], far_weights[...], NT, preferred_element_type=jnp.float32
            )
        ).astype(jnp.bfloat16)

    near_copy.wait()
    far_copy.wait()


VMEM = pl.BlockSpec(memory_space=pltpu.VMEM)
ANY = pl.BlockSpec(memory_space=pl.ANY)


def on_device(weight_delta, rollout_copy, cached_inputs):
    row_count, piece_width = weight_delta.shape
    full_width = rollout_copy.shape[2]
    token_count = cached_inputs.shape[0]
    half_width = full_width // 2
    piece = weight_delta.T
    tokens = pltpu.with_memory_space_constraint(cached_inputs, pltpu.VMEM)
    held = pltpu.with_memory_space_constraint(rollout_copy[0], pltpu.VMEM)

    far_piece = send(piece, dz=1)
    near = [piece] + [send(piece, dy=step) for step in STEPS]
    near_swapped = send(jnp.concatenate(near), dc=1)
    far = [far_piece] + [send(far_piece, dy=step) for step in STEPS]
    far_swapped = send(jnp.concatenate(far), dc=1)

    flops = 2 * token_count * row_count * half_width
    near_weights, partial = pl.pallas_call(
        first_kernel,
        out_shape=(
            pltpu.VMEM((row_count, half_width), jnp.bfloat16),
            pltpu.VMEM((token_count, row_count), jnp.float32),
        ),
        in_specs=[VMEM] * 7,
        out_specs=(VMEM, VMEM),
        scratch_shapes=[pltpu.VMEM((half_width, row_count), jnp.bfloat16)],
        compiler_params=pltpu.CompilerParams(vmem_limit_bytes=16 * 2**20),
        cost_estimate=pl.CostEstimate(flops=flops, bytes_accessed=8 * 2**20, transcendentals=0),
    )(*near, near_swapped, held, tokens)
    renewed, result = pl.pallas_call(
        second_kernel,
        out_shape=(
            jax.ShapeDtypeStruct((row_count, full_width), jnp.bfloat16),
            jax.ShapeDtypeStruct((token_count, row_count), jnp.bfloat16),
        ),
        in_specs=[VMEM] * 9,
        out_specs=(ANY, VMEM),
        scratch_shapes=[
            pltpu.VMEM((half_width, row_count), jnp.bfloat16),
            pltpu.VMEM((row_count, half_width), jnp.bfloat16),
            pltpu.SemaphoreType.DMA,
            pltpu.SemaphoreType.DMA,
        ],
        compiler_params=pltpu.CompilerParams(vmem_limit_bytes=16 * 2**20),
        cost_estimate=pl.CostEstimate(flops=flops, bytes_accessed=8 * 2**20, transcendentals=0),
    )(*far, far_swapped, held, tokens, near_weights, partial)
    return (renewed[None], result)


def solution(mesh):
    placed = (P("tp", "replica"), P("replica", "tp", None), P("replica", None))
    return jax.shard_map(
        on_device,
        mesh=mesh,
        in_specs=placed,
        out_specs=(P("replica", "tp", None), P("replica", "tp")),
        check_vma=False,
    )
```

```python
import functools

import jax
import jax.numpy as jnp
from jax import lax
from jax.experimental import pallas as pl
from jax.experimental.pallas import tpu as pltpu
from jax.sharding import PartitionSpec as P

TILE = 128
EPSILON = 1e-06
STEPS = (2, 1, 3)
TOKEN_BLOCK = 512

NT = (((1,), (1,)), ((), ()))


def moved(dz=0, dy=0, dc=0):
    pairs = []
    for source in range(16):
        z, y, core = source >> 3, (source >> 1) & 3, source & 1
        pairs.append((source, ((z + dz) % 2) * 8 + ((y + dy) % 4) * 2 + (core + dc) % 2))
    return pairs


def send(value, **offset):
    return lax.ppermute(value, "replica", moved(**offset))


def whereabouts():
    replica = lax.axis_index("replica")
    return replica >> 3, (replica >> 1) & 3, replica & 1


def renew_half(place, pieces, swapped, held, delta, weights, half):
    piece_rows = pieces[0].shape[0]
    half_width = delta.shape[0]
    _, y, core = place
    for index, step in enumerate((0,) + STEPS):
        chip = lax.rem(y + 4 - step, 4)
        base = chip * (2 * piece_rows)
        mine = pl.multiple_of(base + core * piece_rows, 64)
        other = pl.multiple_of(base + (1 - core) * piece_rows, 64)
        delta[pl.ds(mine, piece_rows), :] = pieces[index][...]
        delta[pl.ds(other, piece_rows), :] = swapped[index * piece_rows : (index + 1) * piece_rows, :]
    row = lax.broadcasted_iota(jnp.int32, (TILE, TILE), 0)
    col = lax.broadcasted_iota(jnp.int32, (TILE, TILE), 1)
    identity = (row == col).astype(jnp.bfloat16)
    start = half * half_width
    for t in range(half_width // TILE):
        tile = delta[t * TILE : (t + 1) * TILE, :].astype(jnp.float32)
        scale = jnp.max(jnp.abs(tile), axis=(0, 1), keepdims=True) + EPSILON
        normalized = (tile / scale).astype(jnp.bfloat16)
        turned = lax.dot_general(identity, normalized, NT, preferred_element_type=jnp.float32)
        columns = pl.ds(pl.multiple_of(start + t * TILE, TILE), TILE)
        fresh = held[:, columns].astype(jnp.float32) + turned * scale
        weights[:, t * TILE : (t + 1) * TILE] = fresh.astype(jnp.bfloat16)


def first_kernel(p0, p1, p2, p3, swapped, held, tokens, weights, partial, delta):
    place = whereabouts()
    half = place[0]
    renew_half(place, (p0, p1, p2, p3), swapped, held, delta, weights, half)
    width = weights.shape[1]
    columns = pl.ds(pl.multiple_of(half * width, TILE), width)

    @pl.loop(0, tokens.shape[0] // TOKEN_BLOCK)
    def _(block):
        rows = pl.ds(pl.multiple_of(block * TOKEN_BLOCK, TOKEN_BLOCK), TOKEN_BLOCK)
        partial[rows, :] = lax.dot_general(
            tokens[rows, columns], weights[...], NT, preferred_element_type=jnp.float32
        )


def second_kernel(
    p0, p1, p2, p3, swapped, held, tokens, near_weights, partial,
    renewed, result, delta, far_weights, near_sem, far_sem,
):
    place = whereabouts()
    near, far = place[0], 1 - place[0]
    width = far_weights.shape[1]
    near_columns = pl.ds(pl.multiple_of(near * width, TILE), width)
    far_columns = pl.ds(pl.multiple_of(far * width, TILE), width)
    near_copy = pltpu.make_async_copy(near_weights, renewed.at[:, near_columns], near_sem)
    near_copy.start()
    renew_half(place, (p0, p1, p2, p3), swapped, held, delta, far_weights, far)
    far_copy = pltpu.make_async_copy(far_weights, renewed.at[:, far_columns], far_sem)
    far_copy.start()

    @pl.loop(0, tokens.shape[0] // TOKEN_BLOCK)
    def _(block):
        rows = pl.ds(pl.multiple_of(block * TOKEN_BLOCK, TOKEN_BLOCK), TOKEN_BLOCK)
        result[rows, :] = (
            partial[rows, :]
            + lax.dot_general(
                tokens[rows, far_columns], far_weights[...], NT, preferred_element_type=jnp.float32
            )
        ).astype(jnp.bfloat16)

    near_copy.wait()
    far_copy.wait()


def stage_kernel(piece, staged, sem):
    copy = pltpu.make_async_copy(piece, staged, sem)
    copy.start()
    copy.wait()


VMEM = pl.BlockSpec(memory_space=pltpu.VMEM)
ANY = pl.BlockSpec(memory_space=pl.ANY)


def on_device(weight_delta, rollout_copy, cached_inputs):
    row_count, piece_width = weight_delta.shape
    full_width = rollout_copy.shape[2]
    token_count = cached_inputs.shape[0]
    half_width = full_width // 2
    piece = weight_delta.T
    tokens = pltpu.with_memory_space_constraint(cached_inputs, pltpu.VMEM)
    held = pltpu.with_memory_space_constraint(rollout_copy[0], pltpu.VMEM)

    far_piece = send(piece, dz=1)
    staged = pl.pallas_call(
        stage_kernel,
        out_shape=pltpu.VMEM(piece.shape, piece.dtype),
        in_specs=[ANY],
        out_specs=VMEM,
        scratch_shapes=[pltpu.SemaphoreType.DMA],
        compiler_params=pltpu.CompilerParams(vmem_limit_bytes=2**20),
        cost_estimate=pl.CostEstimate(flops=10**10, bytes_accessed=24 * 2**20, transcendentals=0),
    )(pltpu.with_memory_space_constraint(piece, pltpu.HBM))
    near = [staged] + [send(staged, dy=step) for step in STEPS]
    near_swapped = send(jnp.concatenate(near), dc=1)
    far = [far_piece] + [send(far_piece, dy=step) for step in STEPS]
    far_swapped = send(jnp.concatenate(far), dc=1)

    flops = 2 * token_count * row_count * half_width
    near_weights, partial = pl.pallas_call(
        first_kernel,
        out_shape=(
            pltpu.VMEM((row_count, half_width), jnp.bfloat16),
            pltpu.VMEM((token_count, row_count), jnp.float32),
        ),
        in_specs=[VMEM] * 7,
        out_specs=(VMEM, VMEM),
        scratch_shapes=[pltpu.VMEM((half_width, row_count), jnp.bfloat16)],
        compiler_params=pltpu.CompilerParams(vmem_limit_bytes=16 * 2**20),
        cost_estimate=pl.CostEstimate(flops=flops, bytes_accessed=8 * 2**20, transcendentals=0),
    )(*near, near_swapped, held, tokens)
    renewed, result = pl.pallas_call(
        second_kernel,
        out_shape=(
            jax.ShapeDtypeStruct((row_count, full_width), jnp.bfloat16),
            jax.ShapeDtypeStruct((token_count, row_count), jnp.bfloat16),
        ),
        in_specs=[VMEM] * 9,
        out_specs=(ANY, VMEM),
        scratch_shapes=[
            pltpu.VMEM((half_width, row_count), jnp.bfloat16),
            pltpu.VMEM((row_count, half_width), jnp.bfloat16),
            pltpu.SemaphoreType.DMA,
            pltpu.SemaphoreType.DMA,
        ],
        compiler_params=pltpu.CompilerParams(vmem_limit_bytes=16 * 2**20),
        cost_estimate=pl.CostEstimate(flops=flops, bytes_accessed=8 * 2**20, transcendentals=0),
    )(*far, far_swapped, held, tokens, near_weights, partial)
    return (renewed[None], result)


def solution(mesh):
    placed = (P("tp", "replica"), P("replica", "tp", None), P("replica", None))
    return jax.shard_map(
        on_device,
        mesh=mesh,
        in_specs=placed,
        out_specs=(P("replica", "tp", None), P("replica", "tp")),
        check_vma=False,
    )
```

```python
import functools

import jax
import jax.numpy as jnp
from jax import lax
from jax.experimental import pallas as pl
from jax.experimental.pallas import tpu as pltpu
from jax.sharding import PartitionSpec as P

TILE = 128
EPSILON = 1e-06
TOKEN_BLOCK = 512
STEPS = (0, 2, 1, 3)
CHIP_COLUMNS = 5 * TILE
WHOLE = 2 * TILE
REST = 3 * TILE

NT = (((1,), (1,)), ((), ()))
VMEM = pl.BlockSpec(memory_space=pltpu.VMEM)
ANY = pl.BlockSpec(memory_space=pl.ANY)


def moved(dz=0, dy=0, dc=0):
    pairs = []
    for source in range(16):
        z, y, core = source >> 3, (source >> 1) & 3, source & 1
        pairs.append((source, ((z + dz) % 2) * 8 + ((y + dy) % 4) * 2 + (core + dc) % 2))
    return pairs


def send(value, **offset):
    return lax.ppermute(value, "replica", moved(**offset))


def anchor_kernel(out):
    out[...] = jnp.zeros_like(out)


def chip_start(slot, half_width):
    replica = lax.axis_index("replica")
    half, y = replica >> 3, (replica >> 1) & 3
    chip = lax.rem(y + 4 - STEPS[slot % 4], 4)
    side = half if slot < 4 else 1 - half
    return side * half_width + chip * CHIP_COLUMNS


def renew(delta_tiles, starts, width, held, weights, renewed, sems):
    row = lax.broadcasted_iota(jnp.int32, (TILE, TILE), 0)
    col = lax.broadcasted_iota(jnp.int32, (TILE, TILE), 1)
    identity = (row == col).astype(jnp.bfloat16)
    copies = []
    for slot, start in enumerate(starts):
        for t in range(width // TILE):
            tile = delta_tiles(slot, t).astype(jnp.float32)
            scale = jnp.max(jnp.abs(tile), axis=(0, 1), keepdims=True) + EPSILON
            normalized = (tile / scale).astype(jnp.bfloat16)
            turned = lax.dot_general(identity, normalized, NT, preferred_element_type=jnp.float32)
            columns = pl.ds(pl.multiple_of(start + t * TILE, TILE), TILE)
            fresh = held[:, columns].astype(jnp.float32) + turned * scale
            at = slot * width + t * TILE
            weights[:, at : at + TILE] = fresh.astype(jnp.bfloat16)
        copies.append(
            pltpu.make_async_copy(
                weights.at[:, pl.ds(slot * width, width)],
                renewed.at[:, pl.ds(pl.multiple_of(start, TILE), width)],
                sems.at[slot],
            )
        )
        copies[-1].start()
    return copies


def products(starts, width, tokens, weights):
    for block in range(tokens.shape[0] // TOKEN_BLOCK):
        rows = pl.ds(block * TOKEN_BLOCK, TOKEN_BLOCK)
        left = jnp.concatenate(
            [tokens[rows, pl.ds(pl.multiple_of(start, TILE), width)] for start in starts], axis=1
        )
        yield block, rows, lax.dot_general(left, weights[...], NT, preferred_element_type=jnp.float32)


def whole_kernel(slots, first, *refs):
    pieces, (held, tokens, before), refs = refs[: len(slots)], refs[len(slots) : len(slots) + 3], refs[len(slots) + 3 :]
    if not first:
        refs = refs[1:]
    renewed, total, weights, sems = refs
    core = lax.axis_index("replica") & 1
    starts = [chip_start(slot, tokens.shape[1] // 2) + core * REST for slot in slots]

    def delta_tiles(index, t):
        return pieces[index][pl.ds(pl.multiple_of(core * (TILE // 2) + t * TILE, TILE // 2), TILE), :]

    copies = renew(delta_tiles, starts, WHOLE, held, weights, renewed, sems)
    for _, rows, product in products(starts, WHOLE, tokens, weights):
        total[rows, :] = product if first else before[rows, :] + product
    for copy in copies:
        copy.wait()


def rest_kernel(slots, *refs):
    count = len(slots)
    pieces, (others, held, tokens, before, _) = refs[:count], refs[count : count + 5]
    renewed, result, delta, weights, result_block, sems, result_sems = refs[count + 5 :]
    core = lax.axis_index("replica") & 1
    rows_each = pieces[0].shape[0]
    half_tile = TILE // 2
    starts = [chip_start(slot, tokens.shape[1] // 2) + (1 - core) * WHOLE for slot in slots]
    for index in range(count):
        own_to = pl.multiple_of(index * REST + core * rows_each, half_tile)
        other_to = pl.multiple_of(index * REST + (1 - core) * half_tile, half_tile)
        own_from = pl.multiple_of((1 - core) * WHOLE, half_tile)
        delta[pl.ds(own_to, half_tile), :] = pieces[index][pl.ds(own_from, half_tile), :]
        delta[pl.ds(other_to, rows_each), :] = others[index * rows_each : (index + 1) * rows_each, :]

    def delta_tiles(index, t):
        return delta[index * REST + t * TILE : index * REST + (t + 1) * TILE, :]

    copies = renew(delta_tiles, starts, REST, held, weights, renewed, sems)
    for block, rows, product in products(starts, REST, tokens, weights):
        result_block[rows, :] = (before[rows, :] + product).astype(jnp.bfloat16)
        copies.append(
            pltpu.make_async_copy(result_block.at[rows, :], result.at[rows, :], result_sems.at[block])
        )
        copies[-1].start()
    for copy in copies:
        copy.wait()


def call_kernel(kernel, operands, specs, total, total_spec, aliases, scratch, held, tokens, width):
    return pl.pallas_call(
        kernel,
        out_shape=(jax.ShapeDtypeStruct((held.shape[0], tokens.shape[1]), jnp.bfloat16), total),
        in_specs=specs,
        out_specs=(ANY, total_spec),
        scratch_shapes=scratch,
        input_output_aliases=aliases,
        compiler_params=pltpu.CompilerParams(vmem_limit_bytes=12 * 2**20),
        cost_estimate=pl.CostEstimate(
            flops=4 * tokens.shape[0] * held.shape[0] * width, bytes_accessed=2 * 2**20, transcendentals=0
        ),
    )(*operands)


def whole_part(slots, pieces, held, tokens, before):
    first = not isinstance(before, (tuple, list))
    width = len(slots) * WHOLE
    operands = [*pieces, held, tokens]
    specs = [VMEM] * len(operands)
    aliases = {}
    if first:
        operands.append(before)
        specs.append(ANY)
    else:
        renewed, partial = before
        operands += [partial, renewed]
        specs += [VMEM, ANY]
        aliases = {len(operands) - 2: 1, len(operands) - 1: 0}
    scratch = [
        pltpu.VMEM((held.shape[0], width), jnp.bfloat16),
        pltpu.SemaphoreType.DMA((len(slots),)),
    ]
    total = pltpu.VMEM((tokens.shape[0], held.shape[0]), jnp.float32)
    kernel = functools.partial(whole_kernel, slots, first)
    return call_kernel(kernel, operands, specs, total, VMEM, aliases, scratch, held, tokens, width)


def rest_part(slots, pieces, others, held, tokens, before):
    renewed, partial = before
    width = len(slots) * REST
    operands = [*pieces, others, held, tokens, partial, renewed]
    specs = [VMEM] * (len(operands) - 1) + [ANY]
    scratch = [
        pltpu.VMEM((width, held.shape[0]), jnp.bfloat16),
        pltpu.VMEM((held.shape[0], width), jnp.bfloat16),
        pltpu.VMEM((tokens.shape[0], held.shape[0]), jnp.bfloat16),
        pltpu.SemaphoreType.DMA((len(slots),)),
        pltpu.SemaphoreType.DMA((tokens.shape[0] // TOKEN_BLOCK,)),
    ]
    total = jax.ShapeDtypeStruct((tokens.shape[0], held.shape[0]), jnp.bfloat16)
    kernel = functools.partial(rest_kernel, slots)
    return call_kernel(
        kernel, operands, specs, total, ANY, {len(operands) - 1: 0}, scratch, held, tokens, width
    )


def on_device(weight_delta, rollout_copy, cached_inputs):
    piece = weight_delta.T
    tokens = pltpu.with_memory_space_constraint(cached_inputs, pltpu.VMEM)
    held = pltpu.with_memory_space_constraint(rollout_copy[0], pltpu.VMEM)

    anchor = pl.pallas_call(
        anchor_kernel,
        out_shape=pltpu.VMEM((8, 128), jnp.float32),
        out_specs=VMEM,
        compiler_params=pltpu.CompilerParams(vmem_limit_bytes=2**20),
        cost_estimate=pl.CostEstimate(flops=10**10, bytes_accessed=24 * 2**20, transcendentals=0),
    )()
    own, anchor = lax.optimization_barrier((piece, anchor))
    far_piece = send(piece, dz=1)
    near = [own] + [send(own, dy=step) for step in STEPS[1:]]
    far = [far_piece] + [send(far_piece, dy=step) for step in STEPS[1:]]
    done = whole_part((0, 1, 2, 3), near, held, tokens, anchor)
    near, far, done = lax.optimization_barrier((near, far, done))
    others = send(jnp.concatenate(near + far), dc=1)
    done = whole_part((4, 5, 6, 7), far, held, tokens, done)
    renewed, result = rest_part(tuple(range(8)), near + far, others, held, tokens, done)
    return (renewed[None], result)


def solution(mesh):
    placed = (P("tp", "replica"), P("replica", "tp", None), P("replica", None))
    return jax.shard_map(
        on_device,
        mesh=mesh,
        in_specs=placed,
        out_specs=(P("replica", "tp", None), P("replica", "tp")),
        check_vma=False,
    )
```

```python
import functools

import jax
import jax.numpy as jnp
from jax import lax
from jax.experimental import pallas as pl
from jax.experimental.pallas import tpu as pltpu
from jax.sharding import PartitionSpec as P

TILE = 128
EPSILON = 1e-06
TOKEN_BLOCK = 512
STEPS = ((0, 0), (1, 2), (2, 1), (3, 3))
OTHER_SLOT = (0, 2, 1, 3)
CHIP_COLUMNS = 5 * TILE
WHOLE = 2 * TILE
REST = 3 * TILE

NT = (((1,), (1,)), ((), ()))
VMEM = pl.BlockSpec(memory_space=pltpu.VMEM)
ANY = pl.BlockSpec(memory_space=pl.ANY)


def moved(dz=0, dy=(0, 0), dc=0):
    pairs = []
    for source in range(16):
        z, y, core = source >> 3, (source >> 1) & 3, source & 1
        pairs.append((source, (z ^ dz) * 8 + (y ^ dy[core]) * 2 + (core ^ dc)))
    return pairs


def send(value, **offset):
    return lax.ppermute(value, "replica", moved(**offset))


def anchor_kernel(out):
    out[...] = jnp.zeros_like(out)


def chip_start(slot, far, half_width):
    replica = lax.axis_index("replica")
    half, y = replica >> 3, (replica >> 1) & 3
    step = STEPS[slot]
    chip = y ^ (step[0] + (replica & 1) * (step[1] - step[0]))
    side = 1 - half if far else half
    return side * half_width + chip * CHIP_COLUMNS


def renew(delta, spans, held, weights, renewed, sems):
    row = lax.broadcasted_iota(jnp.int32, (TILE, TILE), 0)
    col = lax.broadcasted_iota(jnp.int32, (TILE, TILE), 1)
    identity = (row == col).astype(jnp.bfloat16)
    copies, at = [], 0
    for slot, (start, width) in enumerate(spans):
        for t in range(width // TILE):
            tile = delta[at + t * TILE : at + (t + 1) * TILE, :].astype(jnp.float32)
            scale = jnp.max(jnp.abs(tile), axis=(0, 1), keepdims=True) + EPSILON
            normalized = (tile / scale).astype(jnp.bfloat16)
            turned = lax.dot_general(identity, normalized, NT, preferred_element_type=jnp.float32)
            columns = pl.ds(pl.multiple_of(start + t * TILE, TILE), TILE)
            fresh = held[:, columns].astype(jnp.float32) + turned * scale
            weights[:, at + t * TILE : at + (t + 1) * TILE] = fresh.astype(jnp.bfloat16)
        copies.append(
            pltpu.make_async_copy(
                weights.at[:, pl.ds(at, width)],
                renewed.at[:, pl.ds(pl.multiple_of(start, TILE), width)],
                sems.at[slot],
            )
        )
        copies[-1].start()
        at += width
    return copies


def products(spans, tokens, weights):
    for block in range(tokens.shape[0] // TOKEN_BLOCK):
        rows = pl.ds(block * TOKEN_BLOCK, TOKEN_BLOCK)
        left = jnp.concatenate(
            [tokens[rows, pl.ds(pl.multiple_of(start, TILE), width)] for start, width in spans], axis=1
        )
        yield block, rows, lax.dot_general(left, weights[...], NT, preferred_element_type=jnp.float32)


def place_whole(delta, at, core, mine):
    delta[at : at + WHOLE, :] = jnp.where(core == 0, mine[:WHOLE, :], mine[TILE // 2 :, :])


def place_rest(delta, at, core, mine, other):
    end, half_tile = at + REST, TILE // 2
    delta[at : at + half_tile, :] = jnp.where(core == 0, mine[WHOLE:, :], other[:half_tile, :])
    delta[at + half_tile : end - half_tile, :] = jnp.where(
        core == 0, other[: WHOLE, :], other[half_tile:, :]
    )
    delta[end - half_tile : end, :] = jnp.where(core == 0, other[WHOLE:, :], mine[:half_tile, :])


def add_products(first, spans, tokens, weights, before, total):
    for _, rows, product in products(spans, tokens, weights):
        total[rows, :] = product if first else before[rows, :] + product


def whole_kernel(slots, first, *refs):
    count = len(slots)
    pieces, (held, tokens, before), refs = refs[:count], refs[count : count + 3], refs[count + 3 :]
    renewed, total, delta, weights, sems = refs[-5:]
    core = lax.axis_index("replica") & 1
    spans = []
    for index, slot in enumerate(slots):
        place_whole(delta, index * WHOLE, core, pieces[index][...])
        spans.append((chip_start(slot % 4, slot >= 4, tokens.shape[1] // 2) + core * REST, WHOLE))
    copies = renew(delta, spans, held, weights, renewed, sems)
    add_products(first, spans, tokens, weights, before, total)
    for copy in copies:
        copy.wait()


def rest_kernel(slots, last, *refs):
    count = len(slots)
    pieces, (others, held, tokens, before, _), refs = refs[:count], refs[count : count + 5], refs[count + 5 :]
    renewed, total, delta, weights = refs[:4]
    sems = refs[5 if last else 4]
    core = lax.axis_index("replica") & 1
    rows = pieces[0].shape[0]
    spans = []
    for index, slot in enumerate(slots):
        other = index - slot % 4 + OTHER_SLOT[slot % 4]
        place_rest(delta, index * REST, core, pieces[index][...], others[other * rows : (other + 1) * rows, :])
        spans.append((chip_start(slot % 4, slot >= 4, tokens.shape[1] // 2) + (1 - core) * WHOLE, REST))
    copies = renew(delta, spans, held, weights, renewed, sems)
    for block, rows, product in products(spans, tokens, weights):
        if not last:
            total[rows, :] = before[rows, :] + product
            continue
        result_block, result_sems = refs[4], refs[6]
        result_block[rows, :] = (before[rows, :] + product).astype(jnp.bfloat16)
        copies.append(
            pltpu.make_async_copy(result_block.at[rows, :], total.at[rows, :], result_sems.at[block])
        )
        copies[-1].start()
    for copy in copies:
        copy.wait()


def whole_part(slots, pieces, held, tokens, before):
    first = not isinstance(before, (tuple, list))
    kernel = functools.partial(whole_kernel, slots, first)
    return run_kernel(kernel, pieces, held, tokens, before, 2 * len(slots), len(slots))


def rest_part(slots, pieces, others, held, tokens, before, last=False):
    kernel = functools.partial(rest_kernel, slots, last)
    return run_kernel(kernel, [*pieces, others], held, tokens, before, 3 * len(slots), len(slots), last)


def run_kernel(kernel, pieces, held, tokens, before, tiles, span_count, last=False):
    width = tiles * TILE
    token_count, row_count = tokens.shape[0], held.shape[0]
    operands = [*pieces, held, tokens]
    specs = [VMEM] * len(operands)
    aliases = {}
    if isinstance(before, (tuple, list)):
        renewed, partial = before
        operands += [partial, renewed]
        specs += [VMEM, ANY]
        aliases = {len(operands) - 1: 0}
        if not last:
            aliases[len(operands) - 2] = 1
    else:
        operands.append(before)
        specs.append(ANY)
    scratch = [
        pltpu.VMEM((width, row_count), jnp.bfloat16),
        pltpu.VMEM((row_count, width), jnp.bfloat16),
    ]
    if last:
        total, total_spec = jax.ShapeDtypeStruct((token_count, row_count), jnp.bfloat16), ANY
        scratch.append(pltpu.VMEM((token_count, row_count), jnp.bfloat16))
    else:
        total, total_spec = pltpu.VMEM((token_count, row_count), jnp.float32), VMEM
    scratch.append(pltpu.SemaphoreType.DMA((span_count,)))
    if last:
        scratch.append(pltpu.SemaphoreType.DMA((token_count // TOKEN_BLOCK,)))
    return pl.pallas_call(
        kernel,
        out_shape=(jax.ShapeDtypeStruct((row_count, tokens.shape[1]), jnp.bfloat16), total),
        in_specs=specs,
        out_specs=(ANY, total_spec),
        scratch_shapes=scratch,
        input_output_aliases=aliases,
        compiler_params=pltpu.CompilerParams(vmem_limit_bytes=12 * 2**20),
        cost_estimate=pl.CostEstimate(
            flops=4 * token_count * row_count * width, bytes_accessed=2 * 2**20, transcendentals=0
        ),
    )(*operands)


def on_device(weight_delta, rollout_copy, cached_inputs):
    piece = weight_delta.T
    tokens = pltpu.with_memory_space_constraint(cached_inputs, pltpu.VMEM)
    held = pltpu.with_memory_space_constraint(rollout_copy[0], pltpu.VMEM)

    anchor = pl.pallas_call(
        anchor_kernel,
        out_shape=pltpu.VMEM((8, 128), jnp.float32),
        out_specs=VMEM,
        compiler_params=pltpu.CompilerParams(vmem_limit_bytes=2**20),
        cost_estimate=pl.CostEstimate(flops=10**10, bytes_accessed=24 * 2**20, transcendentals=0),
    )()
    own, anchor = lax.optimization_barrier((piece, anchor))
    far_piece = send(piece, dz=1)
    near = [own] + [send(own, dy=step) for step in STEPS[1:]]
    far = [far_piece] + [send(far_piece, dy=step) for step in STEPS[1:]]
    done = whole_part((0, 1, 2, 3, 4), near + far[:1], held, tokens, anchor)
    near, far, done = lax.optimization_barrier((near, far, done))
    others = send(jnp.concatenate(near + far), dc=1)
    done = whole_part((5, 6, 7), far[1:], held, tokens, done)
    renewed, result = rest_part(tuple(range(8)), near + far, others, held, tokens, done, last=True)
    return (renewed[None], result)


def solution(mesh):
    placed = (P("tp", "replica"), P("replica", "tp", None), P("replica", None))
    return jax.shard_map(
        on_device,
        mesh=mesh,
        in_specs=placed,
        out_specs=(P("replica", "tp", None), P("replica", "tp")),
        check_vma=False,
    )
```

```python
import functools

import jax
import jax.numpy as jnp
from jax import lax
from jax.experimental import pallas as pl
from jax.experimental.pallas import tpu as pltpu
from jax.sharding import PartitionSpec as P

TILE = 128
EPSILON = 1e-06
TOKEN_BLOCK = 512
STEPS = ((0, 0), (1, 3), (3, 1), (2, 2))
FAR_STEPS = ((0, 0), (1, 2), (2, 1), (3, 3))
OTHER_SLOT = (0, 2, 1, 3)
CHIP_COLUMNS = 5 * TILE
WHOLE = 2 * TILE
REST = 3 * TILE

NT = (((1,), (1,)), ((), ()))
VMEM = pl.BlockSpec(memory_space=pltpu.VMEM)
ANY = pl.BlockSpec(memory_space=pl.ANY)


def moved(dz=0, dy=(0, 0), dc=0):
    pairs = []
    for source in range(16):
        z, y, core = source >> 3, (source >> 1) & 3, source & 1
        pairs.append((source, (z ^ dz) * 8 + (y ^ dy[core]) * 2 + (core ^ dc)))
    return pairs


def send(value, **offset):
    return lax.ppermute(value, "replica", moved(**offset))


def anchor_kernel(out):
    out[...] = jnp.zeros_like(out)


def chip_start(slot, far, half_width):
    replica = lax.axis_index("replica")
    half, y = replica >> 3, (replica >> 1) & 3
    step = (FAR_STEPS if far else STEPS)[slot]
    chip = y ^ (step[0] + (replica & 1) * (step[1] - step[0]))
    side = 1 - half if far else half
    return side * half_width + chip * CHIP_COLUMNS


def renew(delta, spans, held, weights, renewed, sems):
    row = lax.broadcasted_iota(jnp.int32, (TILE, TILE), 0)
    col = lax.broadcasted_iota(jnp.int32, (TILE, TILE), 1)
    identity = (row == col).astype(jnp.bfloat16)
    copies, at = [], 0
    for slot, (start, width) in enumerate(spans):
        for t in range(width // TILE):
            tile = delta[at + t * TILE : at + (t + 1) * TILE, :].astype(jnp.float32)
            scale = jnp.max(jnp.abs(tile), axis=(0, 1), keepdims=True) + EPSILON
            normalized = (tile / scale).astype(jnp.bfloat16)
            turned = lax.dot_general(identity, normalized, NT, preferred_element_type=jnp.float32)
            columns = pl.ds(pl.multiple_of(start + t * TILE, TILE), TILE)
            fresh = held[:, columns].astype(jnp.float32) + turned * scale
            weights[:, at + t * TILE : at + (t + 1) * TILE] = fresh.astype(jnp.bfloat16)
        copies.append(
            pltpu.make_async_copy(
                weights.at[:, pl.ds(at, width)],
                renewed.at[:, pl.ds(pl.multiple_of(start, TILE), width)],
                sems.at[slot],
            )
        )
        copies[-1].start()
        at += width
    return copies


def products(spans, tokens, weights):
    for block in range(tokens.shape[0] // TOKEN_BLOCK):
        rows = pl.ds(block * TOKEN_BLOCK, TOKEN_BLOCK)
        left = jnp.concatenate(
            [tokens[rows, pl.ds(pl.multiple_of(start, TILE), width)] for start, width in spans], axis=1
        )
        yield block, rows, lax.dot_general(left, weights[...], NT, preferred_element_type=jnp.float32)


def place_whole(delta, at, core, mine):
    delta[at : at + WHOLE, :] = jnp.where(core == 0, mine[:WHOLE, :], mine[TILE // 2 :, :])


def place_rest(delta, at, core, mine, other):
    end, half_tile = at + REST, TILE // 2
    delta[at : at + half_tile, :] = jnp.where(core == 0, mine[WHOLE:, :], other[:half_tile, :])
    delta[at + half_tile : end - half_tile, :] = jnp.where(
        core == 0, other[: WHOLE, :], other[half_tile:, :]
    )
    delta[end - half_tile : end, :] = jnp.where(core == 0, other[WHOLE:, :], mine[:half_tile, :])


def add_products(first, spans, tokens, weights, before, total):
    for _, rows, product in products(spans, tokens, weights):
        total[rows, :] = product if first else before[rows, :] + product


def whole_kernel(slots, first, *refs):
    count = len(slots)
    pieces, (held, tokens, before), refs = refs[:count], refs[count : count + 3], refs[count + 3 :]
    renewed, total, delta, weights, sems = refs[-5:]
    core = lax.axis_index("replica") & 1
    spans = []
    for index, slot in enumerate(slots):
        place_whole(delta, index * WHOLE, core, pieces[index][...])
        spans.append((chip_start(slot % 4, slot >= 4, tokens.shape[1] // 2) + core * REST, WHOLE))
    copies = renew(delta, spans, held, weights, renewed, sems)
    add_products(first, spans, tokens, weights, before, total)
    for copy in copies:
        copy.wait()


def rest_kernel(slots, last, *refs):
    count = len(slots)
    pieces, (others, held, tokens, before, _), refs = refs[:count], refs[count : count + 5], refs[count + 5 :]
    renewed, total, delta, weights = refs[:4]
    sems = refs[5 if last else 4]
    core = lax.axis_index("replica") & 1
    rows = pieces[0].shape[0]
    spans = []
    for index, slot in enumerate(slots):
        other = index - slot % 4 + OTHER_SLOT[slot % 4]
        place_rest(delta, index * REST, core, pieces[index][...], others[other * rows : (other + 1) * rows, :])
        spans.append((chip_start(slot % 4, slot >= 4, tokens.shape[1] // 2) + (1 - core) * WHOLE, REST))
    copies = renew(delta, spans, held, weights, renewed, sems)
    for block, rows, product in products(spans, tokens, weights):
        if not last:
            total[rows, :] = before[rows, :] + product
            continue
        result_block, result_sems = refs[4], refs[6]
        result_block[rows, :] = (before[rows, :] + product).astype(jnp.bfloat16)
        copies.append(
            pltpu.make_async_copy(result_block.at[rows, :], total.at[rows, :], result_sems.at[block])
        )
        copies[-1].start()
    for copy in copies:
        copy.wait()


def whole_part(slots, pieces, held, tokens, before):
    first = not isinstance(before, (tuple, list))
    kernel = functools.partial(whole_kernel, slots, first)
    return run_kernel(kernel, pieces, held, tokens, before, 2 * len(slots), len(slots))


def rest_part(slots, pieces, others, held, tokens, before, last=False):
    kernel = functools.partial(rest_kernel, slots, last)
    return run_kernel(kernel, [*pieces, others], held, tokens, before, 3 * len(slots), len(slots), last)


def run_kernel(kernel, pieces, held, tokens, before, tiles, span_count, last=False):
    width = tiles * TILE
    token_count, row_count = tokens.shape[0], held.shape[0]
    operands = [*pieces, held, tokens]
    specs = [VMEM] * len(operands)
    aliases = {}
    if isinstance(before, (tuple, list)):
        renewed, partial = before
        operands += [partial, renewed]
        specs += [VMEM, ANY]
        aliases = {len(operands) - 1: 0}
        if not last:
            aliases[len(operands) - 2] = 1
    else:
        operands.append(before)
        specs.append(ANY)
    scratch = [
        pltpu.VMEM((width, row_count), jnp.bfloat16),
        pltpu.VMEM((row_count, width), jnp.bfloat16),
    ]
    if last:
        total, total_spec = jax.ShapeDtypeStruct((token_count, row_count), jnp.bfloat16), ANY
        scratch.append(pltpu.VMEM((token_count, row_count), jnp.bfloat16))
    else:
        total, total_spec = pltpu.VMEM((token_count, row_count), jnp.float32), VMEM
    scratch.append(pltpu.SemaphoreType.DMA((span_count,)))
    if last:
        scratch.append(pltpu.SemaphoreType.DMA((token_count // TOKEN_BLOCK,)))
    return pl.pallas_call(
        kernel,
        out_shape=(jax.ShapeDtypeStruct((row_count, tokens.shape[1]), jnp.bfloat16), total),
        in_specs=specs,
        out_specs=(ANY, total_spec),
        scratch_shapes=scratch,
        input_output_aliases=aliases,
        compiler_params=pltpu.CompilerParams(vmem_limit_bytes=12 * 2**20),
        cost_estimate=pl.CostEstimate(
            flops=4 * token_count * row_count * width, bytes_accessed=2 * 2**20, transcendentals=0
        ),
    )(*operands)


def on_device(weight_delta, rollout_copy, cached_inputs):
    piece = weight_delta.T
    tokens = pltpu.with_memory_space_constraint(cached_inputs, pltpu.VMEM)
    held = pltpu.with_memory_space_constraint(rollout_copy[0], pltpu.VMEM)

    anchor = pl.pallas_call(
        anchor_kernel,
        out_shape=pltpu.VMEM((8, 128), jnp.float32),
        out_specs=VMEM,
        compiler_params=pltpu.CompilerParams(vmem_limit_bytes=2**20),
        cost_estimate=pl.CostEstimate(flops=10**10, bytes_accessed=24 * 2**20, transcendentals=0),
    )()
    own, anchor = lax.optimization_barrier((piece, anchor))
    far_piece = send(piece, dz=1)
    near = [own] + [send(own, dy=step) for step in STEPS[1:]]
    far = [far_piece] + [send(far_piece, dy=step) for step in FAR_STEPS[1:]]
    done = whole_part((0, 1, 2, 3, 4), near + far[:1], held, tokens, anchor)
    near, far, done = lax.optimization_barrier((near, far, done))
    others = send(jnp.concatenate(near + far), dc=1)
    done = whole_part((5, 6, 7), far[1:], held, tokens, done)
    renewed, result = rest_part(tuple(range(8)), near + far, others, held, tokens, done, last=True)
    return (renewed[None], result)


def solution(mesh):
    placed = (P("tp", "replica"), P("replica", "tp", None), P("replica", None))
    return jax.shard_map(
        on_device,
        mesh=mesh,
        in_specs=placed,
        out_specs=(P("replica", "tp", None), P("replica", "tp")),
        check_vma=False,
    )
```

```python
import functools

import jax
import jax.numpy as jnp
from jax import lax
from jax.experimental import pallas as pl
from jax.experimental.pallas import tpu as pltpu
from jax.sharding import PartitionSpec as P

TILE = 128
EPSILON = 1e-06
TOKEN_BLOCK = 512
STEPS = ((0, 0), (1, 3), (3, 1), (2, 2))
FAR_STEPS = ((0, 0), (3, 2), (2, 3), (1, 1))
OTHER_SLOT = (0, 2, 1, 3)
CHIP_COLUMNS = 5 * TILE
WHOLE = 2 * TILE
REST = 3 * TILE

NT = (((1,), (1,)), ((), ()))
VMEM = pl.BlockSpec(memory_space=pltpu.VMEM)
ANY = pl.BlockSpec(memory_space=pl.ANY)


def moved(dz=0, dy=(0, 0), dc=0):
    pairs = []
    for source in range(16):
        z, y, core = source >> 3, (source >> 1) & 3, source & 1
        pairs.append((source, (z ^ dz) * 8 + (y ^ dy[core]) * 2 + (core ^ dc)))
    return pairs


def send(value, **offset):
    return lax.ppermute(value, "replica", moved(**offset))


def anchor_kernel(out):
    out[...] = jnp.zeros_like(out)


def chip_start(slot, far, half_width):
    replica = lax.axis_index("replica")
    half, y = replica >> 3, (replica >> 1) & 3
    step = (FAR_STEPS if far else STEPS)[slot]
    chip = y ^ (step[0] + (replica & 1) * (step[1] - step[0]))
    side = 1 - half if far else half
    return side * half_width + chip * CHIP_COLUMNS


def renew(delta, spans, held, weights, renewed, sems):
    row = lax.broadcasted_iota(jnp.int32, (TILE, TILE), 0)
    col = lax.broadcasted_iota(jnp.int32, (TILE, TILE), 1)
    identity = (row == col).astype(jnp.bfloat16)
    copies, at = [], 0
    for slot, (start, width) in enumerate(spans):
        for t in range(width // TILE):
            tile = delta[at + t * TILE : at + (t + 1) * TILE, :].astype(jnp.float32)
            scale = jnp.max(jnp.abs(tile), axis=(0, 1), keepdims=True) + EPSILON
            normalized = (tile / scale).astype(jnp.bfloat16)
            turned = lax.dot_general(identity, normalized, NT, preferred_element_type=jnp.float32)
            columns = pl.ds(pl.multiple_of(start + t * TILE, TILE), TILE)
            fresh = held[:, columns].astype(jnp.float32) + turned * scale
            weights[:, at + t * TILE : at + (t + 1) * TILE] = fresh.astype(jnp.bfloat16)
        copies.append(
            pltpu.make_async_copy(
                weights.at[:, pl.ds(at, width)],
                renewed.at[:, pl.ds(pl.multiple_of(start, TILE), width)],
                sems.at[slot],
            )
        )
        copies[-1].start()
        at += width
    return copies


def products(spans, tokens, weights):
    for block in range(tokens.shape[0] // TOKEN_BLOCK):
        rows = pl.ds(block * TOKEN_BLOCK, TOKEN_BLOCK)
        left = jnp.concatenate(
            [tokens[rows, pl.ds(pl.multiple_of(start, TILE), width)] for start, width in spans], axis=1
        )
        yield block, rows, lax.dot_general(left, weights[...], NT, preferred_element_type=jnp.float32)


def place_whole(delta, at, core, mine):
    delta[at : at + WHOLE, :] = jnp.where(core == 0, mine[:WHOLE, :], mine[TILE // 2 :, :])


def place_rest(delta, at, core, mine, other):
    end, half_tile = at + REST, TILE // 2
    delta[at : at + half_tile, :] = jnp.where(core == 0, mine[WHOLE:, :], other[:half_tile, :])
    delta[at + half_tile : end - half_tile, :] = jnp.where(
        core == 0, other[: WHOLE, :], other[half_tile:, :]
    )
    delta[end - half_tile : end, :] = jnp.where(core == 0, other[WHOLE:, :], mine[:half_tile, :])


def add_products(first, spans, tokens, weights, before, total):
    for _, rows, product in products(spans, tokens, weights):
        total[rows, :] = product if first else before[rows, :] + product


def whole_kernel(slots, first, *refs):
    count = len(slots)
    pieces, (held, tokens, before), refs = refs[:count], refs[count : count + 3], refs[count + 3 :]
    renewed, total, delta, weights, sems = refs[-5:]
    core = lax.axis_index("replica") & 1
    spans = []
    for index, slot in enumerate(slots):
        place_whole(delta, index * WHOLE, core, pieces[index][...])
        spans.append((chip_start(slot % 4, slot >= 4, tokens.shape[1] // 2) + core * REST, WHOLE))
    copies = renew(delta, spans, held, weights, renewed, sems)
    add_products(first, spans, tokens, weights, before, total)
    for copy in copies:
        copy.wait()


def rest_kernel(slots, last, *refs):
    count = len(slots)
    pieces, (others, held, tokens, before, _), refs = refs[:count], refs[count : count + 5], refs[count + 5 :]
    renewed, total, delta, weights = refs[:4]
    sems = refs[5 if last else 4]
    core = lax.axis_index("replica") & 1
    rows = pieces[0].shape[0]
    spans = []
    for index, slot in enumerate(slots):
        other = index - slot % 4 + OTHER_SLOT[slot % 4]
        place_rest(delta, index * REST, core, pieces[index][...], others[other * rows : (other + 1) * rows, :])
        spans.append((chip_start(slot % 4, slot >= 4, tokens.shape[1] // 2) + (1 - core) * WHOLE, REST))
    copies = renew(delta, spans, held, weights, renewed, sems)
    for block, rows, product in products(spans, tokens, weights):
        if not last:
            total[rows, :] = before[rows, :] + product
            continue
        result_block, result_sems = refs[4], refs[6]
        result_block[rows, :] = (before[rows, :] + product).astype(jnp.bfloat16)
        copies.append(
            pltpu.make_async_copy(result_block.at[rows, :], total.at[rows, :], result_sems.at[block])
        )
        copies[-1].start()
    for copy in copies:
        copy.wait()


def whole_part(slots, pieces, held, tokens, before):
    first = not isinstance(before, (tuple, list))
    kernel = functools.partial(whole_kernel, slots, first)
    return run_kernel(kernel, pieces, held, tokens, before, 2 * len(slots), len(slots))


def rest_part(slots, pieces, others, held, tokens, before, last=False):
    kernel = functools.partial(rest_kernel, slots, last)
    return run_kernel(kernel, [*pieces, others], held, tokens, before, 3 * len(slots), len(slots), last)


def run_kernel(kernel, pieces, held, tokens, before, tiles, span_count, last=False):
    width = tiles * TILE
    token_count, row_count = tokens.shape[0], held.shape[0]
    operands = [*pieces, held, tokens]
    specs = [VMEM] * len(operands)
    aliases = {}
    if isinstance(before, (tuple, list)):
        renewed, partial = before
        operands += [partial, renewed]
        specs += [VMEM, ANY]
        aliases = {len(operands) - 1: 0}
        if not last:
            aliases[len(operands) - 2] = 1
    else:
        operands.append(before)
        specs.append(ANY)
    scratch = [
        pltpu.VMEM((width, row_count), jnp.bfloat16),
        pltpu.VMEM((row_count, width), jnp.bfloat16),
    ]
    if last:
        total, total_spec = jax.ShapeDtypeStruct((token_count, row_count), jnp.bfloat16), ANY
        scratch.append(pltpu.VMEM((token_count, row_count), jnp.bfloat16))
    else:
        total, total_spec = pltpu.VMEM((token_count, row_count), jnp.float32), VMEM
    scratch.append(pltpu.SemaphoreType.DMA((span_count,)))
    if last:
        scratch.append(pltpu.SemaphoreType.DMA((token_count // TOKEN_BLOCK,)))
    return pl.pallas_call(
        kernel,
        out_shape=(jax.ShapeDtypeStruct((row_count, tokens.shape[1]), jnp.bfloat16), total),
        in_specs=specs,
        out_specs=(ANY, total_spec),
        scratch_shapes=scratch,
        input_output_aliases=aliases,
        compiler_params=pltpu.CompilerParams(vmem_limit_bytes=12 * 2**20),
        cost_estimate=pl.CostEstimate(
            flops=4 * token_count * row_count * width, bytes_accessed=2 * 2**20, transcendentals=0
        ),
    )(*operands)


def on_device(weight_delta, rollout_copy, cached_inputs):
    piece = weight_delta.T
    tokens = pltpu.with_memory_space_constraint(cached_inputs, pltpu.VMEM)
    held = pltpu.with_memory_space_constraint(rollout_copy[0], pltpu.VMEM)

    anchor = pl.pallas_call(
        anchor_kernel,
        out_shape=pltpu.VMEM((8, 128), jnp.float32),
        out_specs=VMEM,
        compiler_params=pltpu.CompilerParams(vmem_limit_bytes=2**20),
        cost_estimate=pl.CostEstimate(flops=10**10, bytes_accessed=24 * 2**20, transcendentals=0),
    )()
    own, anchor = lax.optimization_barrier((piece, anchor))
    far_piece = send(piece, dz=1)
    near = [own] + [send(own, dy=step) for step in STEPS[1:]]
    far = [far_piece] + [send(far_piece, dy=step) for step in FAR_STEPS[1:]]
    done = whole_part((0, 1, 2, 3, 4), near + far[:1], held, tokens, anchor)
    near, far, done = lax.optimization_barrier((near, far, done))
    others = send(jnp.concatenate(near + far), dc=1)
    done = whole_part((5, 6, 7), far[1:], held, tokens, done)
    renewed, result = rest_part(tuple(range(8)), near + far, others, held, tokens, done, last=True)
    return (renewed[None], result)


def solution(mesh):
    placed = (P("tp", "replica"), P("replica", "tp", None), P("replica", None))
    return jax.shard_map(
        on_device,
        mesh=mesh,
        in_specs=placed,
        out_specs=(P("replica", "tp", None), P("replica", "tp")),
        check_vma=False,
    )
```
